32 devices in a mesh: dp: 1, ctx: 16 (over z, x, core), tp: 2 (over y).
Axes of the slice: x: 2, y: 2, z: 4, core: 2. Of those that a mesh axis runs over, the one named last changes fastest.
Arguments:
- query: bfloat16 [1, 2048, 8192], P('dp', 'ctx', 'tp'), may hold values from -80 to 80
- key: bfloat16 [1, 2048, 1024], P('dp', 'ctx', 'tp'), may hold values from -6 to 6
- value: bfloat16 [1, 2048, 1024], P('dp', 'ctx', 'tp'), may hold values from -6 to 6
- key_shift: float32 [1, 2048, 1024], P('dp', 'ctx', 'tp'), may hold values from -0.6 to 0.6
- value_shift: float32 [1, 2048, 1024], P('dp', 'ctx', 'tp'), may hold values from -0.6 to 0.6
- doc_ids: int32 [1, 2048], P('dp', 'ctx'), may hold values from 0 to 31, never falling along the last dimension, each value on 1 to 512 neighbouring positions
- target: bfloat16 [1, 2048, 8192], P('dp', 'ctx', 'tp'), may hold values from -160 to 160
Outputs:
- attn: bfloat16 [1, 2048, 8192], P('dp', 'ctx', 'tp')
- new_key_shift: float32 [1, 2048, 1024], P('dp', 'ctx', 'tp')
- new_value_shift: float32 [1, 2048, 1024], P('dp', 'ctx', 'tp')
The draws below stay inside these ranges and needn't reach their ends.
All inputs are finite; a program needn't handle non-finite values.
Results may differ from the reference program's by a relative error of at most 0.005.
Values may be sent and summed in bfloat16 or wider, within the bound.
A program may use at most 128 MiB of HBM per device.

```python
import math
import jax
import jax.numpy as jnp
import numpy as np
from jax import lax

HEADS = 64
KV_HEADS = 8
HEAD = 128
BATCH = 1
SEQ = 2048
DOC_MAX = 512
DOCS = 32


def shared_keys(key):
    shape = (BATCH, SEQ, KV_HEADS, HEAD)
    base = jax.random.truncated_normal(jax.random.fold_in(key, 11), -6.0, 6.0, shape, jnp.float32)
    return base


def draw_key(key, part):
    return shared_keys(key).reshape(BATCH, SEQ, KV_HEADS * HEAD).astype(jnp.bfloat16)


def draw_query(key, part):
    groups = HEADS // KV_HEADS
    shape = (BATCH, SEQ, KV_HEADS, groups, HEAD)
    drawn = jax.random.truncated_normal(jax.random.fold_in(key, 21), -6.0, 6.0, shape, jnp.float32)
    return drawn.reshape(BATCH, SEQ, HEADS * HEAD).astype(jnp.bfloat16)


def draw_target(key, part):
    shape = (BATCH, SEQ, HEADS * HEAD)
    ramp = jnp.exp(jnp.log(3.0) * jnp.arange(SEQ, dtype=jnp.float32) / SEQ)[None, :, None]
    drawn = jax.random.truncated_normal(jax.random.fold_in(key, 31), -5.0, 5.0, shape, jnp.float32)
    return (drawn * ramp).astype(jnp.bfloat16)


def block_levels(own_key, dims, pieces, smallest, top_value):
    gain, own = 1.0, jax.random.fold_in(own_key, 6)
    for position, shards_of in pieces:
        heights = jnp.exp(jax.random.uniform(jax.random.fold_in(own, position), (shards_of,), jnp.float32, smallest / len(pieces), top_value / len(pieces)))
        gain = gain * jnp.repeat(heights, dims[position] // shards_of).reshape([-1 if axis == position else 1 for axis in range(len(dims))])
    return gain


def split_up(count, total, most, lean):
    weights = [(1 << 20) // math.isqrt(rank ** lean) + 1 for rank in range(2, count + 1)]
    rest, counts = total - most - (count - 1), [1] * (count - 1)
    while rest > 0:
        movable = [i for i in range(count - 1) if counts[i] < most]
        whole, budget = sum([weights[i] for i in movable]), rest
        for i in movable:
            addition = min(most - counts[i], max(1, budget * weights[i] // whole), rest)
            counts[i] = counts[i] + addition
            rest = rest - addition
    return np.array([most] + counts)


def uneven(rng, number_of, total, limit, lean):
    if number_of == 2:
        one = jax.random.randint(rng, (), max(1, total - limit), min(limit, total - 1) + 1)
        return jnp.stack([one, total - one])
    tallies = jnp.asarray(split_up(number_of, total, limit, lean), jnp.int32)
    couples = (number_of - 1) // 2
    source_of, taker = tallies[1:1 + 2 * couples:2], tallies[2:2 + 2 * couples:2]
    slack = jnp.minimum(source_of - 1, limit - taker)
    shifted = jax.random.randint(jax.random.fold_in(rng, 1), (couples,), 0, 1 << 20) % (slack + 1)
    tallies = tallies.at[1:1 + 2 * couples:2].set(source_of - shifted).at[2:2 + 2 * couples:2].set(taker + shifted)
    return tallies[jax.random.permutation(jax.random.fold_in(rng, 2), number_of)]


def bell_draw(own_key, dims, spread, limit, shards=(), held_as=jnp.bfloat16):
    gain = block_levels(own_key, dims, shards, -0.22, 0.18) if shards else 1.0
    entries = jax.random.normal(own_key, dims, jnp.float32) * spread * gain
    return jnp.minimum(jnp.maximum(entries, -limit), limit).astype(held_as)


def setup_inputs(seed: int = 0) -> dict:
    seeds = jax.random.split(jax.random.key(seed), 8)
    return {
        "query": draw_query(jax.random.fold_in(seeds[7], 71), 0),
        "key": draw_key(jax.random.fold_in(seeds[7], 71), 0),
        "value": bell_draw(seeds[2], (BATCH, SEQ, KV_HEADS * HEAD), 1.0, 6.0, ((1, 16), (2, 2))),
        "key_shift": bell_draw(seeds[3], (BATCH, SEQ, KV_HEADS * HEAD), 0.1, 0.6, ((1, 16), (2, 2)), jnp.float32),
        "value_shift": bell_draw(seeds[4], (BATCH, SEQ, KV_HEADS * HEAD), 0.1, 0.6, ((1, 16), (2, 2)), jnp.float32),
        "doc_ids": jax.vmap(lambda own: jnp.searchsorted(jnp.cumsum(uneven(own, DOCS, SEQ, DOC_MAX, 2)), jnp.arange(SEQ), side="right"))(jax.random.split(seeds[5], BATCH)).reshape((BATCH, SEQ)).astype(jnp.int32),
        "target": draw_target(jax.random.fold_in(seeds[7], 71), 0),
    }


step_size = 0.1
radius_scale = 0.13

def reference(query, key, value, key_shift, value_shift, doc_ids, target):
    group = HEADS // KV_HEADS
    block = min(512, SEQ)
    width = DOC_MAX + block
    scale = 1.0 / math.sqrt(HEAD)
    key_new = (key.astype(jnp.float32) + key_shift).astype(jnp.bfloat16)
    val_new = (value.astype(jnp.float32) + value_shift).astype(jnp.bfloat16)
    outs = []
    grad_keys = []
    grad_vals = []
    for batch_row in range(BATCH):
        q_all = query[batch_row].reshape(SEQ, KV_HEADS, group, HEAD)
        t_all = target[batch_row].reshape(SEQ, KV_HEADS, group, HEAD)
        k_pad = jnp.concatenate([jnp.zeros((DOC_MAX, KV_HEADS, HEAD), key_new.dtype), key_new[batch_row].reshape(SEQ, KV_HEADS, HEAD)], 0)
        v_pad = jnp.concatenate([jnp.zeros((DOC_MAX, KV_HEADS, HEAD), val_new.dtype), val_new[batch_row].reshape(SEQ, KV_HEADS, HEAD)], 0)
        d_pad = jnp.concatenate([-jnp.ones((DOC_MAX,), jnp.int32), doc_ids[batch_row].astype(jnp.int32)], 0)
        own_docs = doc_ids[batch_row].astype(jnp.int32)

        def one_block(carry, start):
            grad_k, grad_v = carry
            q_blk = lax.dynamic_slice_in_dim(q_all, start, block, 0)
            t_blk = lax.dynamic_slice_in_dim(t_all, start, block, 0)
            k_win = lax.dynamic_slice_in_dim(k_pad, start, width, 0)
            v_win = lax.dynamic_slice_in_dim(v_pad, start, width, 0)
            d_win = lax.dynamic_slice_in_dim(d_pad, start, width, 0)
            d_blk = lax.dynamic_slice_in_dim(own_docs, start, block, 0)
            q_pos = start + jnp.arange(block, dtype=jnp.int32)
            k_pos = start - DOC_MAX + jnp.arange(width, dtype=jnp.int32)
            allowed = (d_win[None, :] == d_blk[:, None]) & (k_pos[None, :] <= q_pos[:, None]) & (k_pos[None, :] >= 0)

            def per_head(items):
                q_head, t_head, k_head, v_head = items
                qf = q_head.astype(jnp.float32)
                tf = t_head.astype(jnp.float32)
                kf = k_head.astype(jnp.float32)
                vf = v_head.astype(jnp.float32)
                scores = jnp.einsum('tgd,wd->gtw', qf, kf) * scale
                scores = jnp.where(allowed[None], scores, -jnp.inf)
                top = lax.optimization_barrier(jnp.max(scores, -1, keepdims=True))
                expo = jnp.exp(scores - top)
                total = lax.optimization_barrier(jnp.sum(expo, -1, keepdims=True))
                expo16 = expo.astype(jnp.bfloat16)
                out = jnp.einsum('gtw,wd->gtd', expo16.astype(jnp.float32), vf) / total
                dprob = jnp.einsum('tgd,wd->gtw', tf, vf)
                delta = lax.optimization_barrier(jnp.sum(jnp.transpose(tf, (1, 0, 2)) * out, -1, keepdims=True))
                prob = expo / total
                ds16 = (prob * (dprob - delta)).astype(jnp.bfloat16)
                prob16 = prob.astype(jnp.bfloat16)
                dk = jnp.einsum('gtw,tgd->wd', ds16.astype(jnp.float32), qf) * scale
                dv = jnp.einsum('gtw,tgd->wd', prob16.astype(jnp.float32), tf)
                return (jnp.transpose(out.astype(jnp.bfloat16), (1, 0, 2)), dk, dv)
            out_blk, dk_blk, dv_blk = lax.map(per_head, (jnp.transpose(q_blk, (1, 0, 2, 3)), jnp.transpose(t_blk, (1, 0, 2, 3)), jnp.transpose(k_win, (1, 0, 2)), jnp.transpose(v_win, (1, 0, 2))))
            old_k = lax.dynamic_slice_in_dim(grad_k, start, width, 0)
            old_v = lax.dynamic_slice_in_dim(grad_v, start, width, 0)
            grad_k = lax.dynamic_update_slice_in_dim(grad_k, old_k + jnp.transpose(dk_blk, (1, 0, 2)), start, 0)
            grad_v = lax.dynamic_update_slice_in_dim(grad_v, old_v + jnp.transpose(dv_blk, (1, 0, 2)), start, 0)
            return ((grad_k, grad_v), jnp.transpose(out_blk, (1, 0, 2, 3)).reshape(block, HEADS * HEAD))
        starts = (jnp.arange(SEQ // block, dtype=jnp.int32) * block).astype(jnp.int32)
        zero_grad = jnp.zeros((DOC_MAX + SEQ, KV_HEADS, HEAD), jnp.float32)
        (grad_k, grad_v), out_blocks = lax.scan(one_block, (zero_grad, zero_grad), starts)
        outs.append(out_blocks.reshape(SEQ, HEADS * HEAD))
        grad_keys.append(grad_k[DOC_MAX:].reshape(SEQ, KV_HEADS * HEAD))
        grad_vals.append(grad_v[DOC_MAX:].reshape(SEQ, KV_HEADS * HEAD))
    attn = jnp.stack(outs, 0)
    grad_key = jnp.stack(grad_keys, 0)
    grad_val = jnp.stack(grad_vals, 0)
    count = BATCH * SEQ * 2 * KV_HEADS * HEAD
    rms = jnp.sqrt((jnp.sum(grad_key * grad_key) + jnp.sum(grad_val * grad_val)) / count + 1e-05)
    moved_key = key_shift + step_size / rms * grad_key
    moved_val = value_shift + step_size / rms * grad_val
    size_sq = lax.optimization_barrier(jnp.sum(moved_key * moved_key, -1, keepdims=True)) + lax.optimization_barrier(jnp.sum(moved_val * moved_val, -1, keepdims=True))
    radius = radius_scale * math.sqrt(2 * KV_HEADS * HEAD)
    factor = jnp.minimum(1.0, radius / jnp.sqrt(size_sq + 1e-06))
    return (attn, moved_key * factor, moved_val * factor)
```

```python
import functools
import math

import jax
import jax.numpy as jnp
from jax import lax
from jax.experimental import pallas as pl
from jax.experimental.pallas import tpu as pltpu
from jax.sharding import PartitionSpec as P

HEADS = 64
KV_HEADS = 8
HEAD = 128
GROUP = HEADS // KV_HEADS
EXTRA = 16
LANES = 128

step_size = 0.1
radius_scale = 0.13

MESH = pl.DeviceIdType.MESH
NT = (((1,), (1,)), ((), ()))


def kernel(
    cfg,
    q_hbm, t_hbm, key_ref, value_ref, ks_ref, vs_ref, doc_ref,
    attn_hbm, nks_ref, nvs_ref,
    q_v, t_v, o_v, buf, bias, p_all, ds_all, acc, gout, gin, stat_mine, stat_in,
    load_sem, out_sem, fs_sem, fr_sem, bs_sem, br_sem, ss_sem, sr_sem,
):
    n_dp, n, n_tp, reach, kvl, tokens, tree = cfg
    total_dev = n_dp * n * n_tp
    slots = reach + 1
    width = slots * tokens
    scale = 1.0 / math.sqrt(HEAD)
    coef = scale * math.log2(math.e)
    me = lax.axis_index("ctx")
    lin = (lax.axis_index("dp") * n + me) * n_tp + lax.axis_index("tp")
    core = lax.rem(me, 2)
    xpos = lax.rem(me // 2, 2)
    mate = me + 1 - 2 * core

    def device_of(linear):
        return {
            "dp": linear // (n * n_tp),
            "ctx": lax.rem(linear // n_tp, n),
            "tp": lax.rem(linear, n_tp),
        }

    barrier = pltpu.get_barrier_semaphore()

    @pl.loop(1, total_dev)
    def _(d):
        pl.semaphore_signal(
            barrier, inc=1, device_id=device_of(lax.rem(lin + d, total_dev)), device_id_type=MESH
        )

    loads = [
        pltpu.make_async_copy(q_hbm, q_v, load_sem.at[0]),
        pltpu.make_async_copy(t_hbm, t_v, load_sem.at[1]),
    ]
    for copy in loads:
        copy.start()

    def rows_of(p):
        return pl.ds(EXTRA + p * tokens, tokens)

    def piece(p):
        return pl.ds(0, EXTRA + tokens) if p == 0 else rows_of(p)

    docs_row = doc_ref[...].astype(jnp.float32)
    buf[0, pl.ds(0, EXTRA), pl.ds(0, tokens)] = jnp.broadcast_to(docs_row, (EXTRA, tokens)).astype(
        jnp.bfloat16
    )
    buf[0, pl.ds(0, EXTRA), pl.ds(HEAD, HEAD)] = jnp.zeros((EXTRA, HEAD), jnp.bfloat16)
    for p in range(kvl):
        cols = pl.ds(p * HEAD, HEAD)
        buf[0, rows_of(p), pl.ds(0, HEAD)] = (
            key_ref[:, cols].astype(jnp.float32) + ks_ref[:, cols]
        ).astype(jnp.bfloat16)
        buf[0, rows_of(p), pl.ds(HEAD, HEAD)] = (
            value_ref[:, cols].astype(jnp.float32) + vs_ref[:, cols]
        ).astype(jnp.bfloat16)
    for k in range(1, slots):
        @pl.when(me < k)
        def _(k=k):
            buf[k] = jnp.zeros(buf.shape[1:], buf.dtype)

    has = {k: me >= k for k in range(1, slots)}

    def fsend(m, p, src, target, slot):
        return pltpu.make_async_remote_copy(
            src_ref=buf.at[src, piece(p)],
            dst_ref=buf.at[slot, piece(p)],
            send_sem=fs_sem.at[m, p],
            recv_sem=fr_sem.at[slot - 1, p],
            device_id={"ctx": target},
            device_id_type=MESH,
        )

    def frecv(slot, p):
        @pl.when(has[slot])
        def _():
            fsend(0, p, 0, me, slot).wait_recv()

    if tree:
        back_in = {
            0: (core == 0) | (me >= 3),
            1: ((core == 0) & (me >= 2)) | (me >= 5),
            2: (xpos == 0) | (me >= 4),
            3: me + 4 < n,
        }
        forward = [
            (me + 4 < n, 0, me + 4, 4),
            ((xpos == 0) | (me >= 4), 4 * xpos, me + 2 - 4 * xpos, 2),
            ((core == 0) | (me >= 2), 2 * core, mate, 1),
            (me >= 2 + 2 * core, 2 + 2 * core, mate, 3),
        ]
        backward = {
            1: (me >= 1, mate, 0),
            3: (me >= 3, mate, 1),
            2: (me >= 2, me + 2 - 4 * xpos, 2),
            4: (me >= 4, me - 4, 3),
        }
    else:
        back_in = {k - 1: me + k < n for k in range(1, slots)}
        forward = [(me + k < n, 0, me + k, k) for k in range(1, slots)]
        backward = {k: (me >= k, me - k, k - 1) for k in range(1, slots)}

    def fstart(m, p, extra=None):
        valid, src, target, slot = forward[m]
        @pl.when(valid if extra is None else valid & extra)
        def _():
            fsend(m, p, src, target, slot).start()

    for i in back_in:
        @pl.when(jnp.logical_not(back_in[i]))
        def _(i=i):
            gin[i] = jnp.zeros(gin.shape[1:], gin.dtype)

    pl.semaphore_wait(barrier, total_dev - 1)

    for p in range(kvl):
        if tree:
            fstart(0, p)
            fstart(1, p, xpos == 0)
            fstart(2, p, core == 0)
        else:
            for m in range(reach):
                fstart(m, p)

    def relay4(p):
        if tree and p < kvl:
            frecv(4, p)
            fstart(1, p, xpos == 1)

    def relay2(p):
        if tree and p < kvl:
            frecv(2, p)
            fstart(2, p, core == 1)
            fstart(3, p)

    def bsend(k, p):
        valid, target, place = backward[k]
        return pltpu.make_async_remote_copy(
            src_ref=gout.at[k - 1, p],
            dst_ref=gin.at[place, p],
            send_sem=bs_sem.at[k - 1, p],
            recv_sem=br_sem.at[place, p],
            device_id={"ctx": target},
            device_id_type=MESH,
        )

    def bstart(k, p):
        @pl.when(backward[k][0])
        def _():
            bsend(k, p).start()

    def brecv(place, p):
        @pl.when(back_in[place])
        def _():
            pltpu.make_async_remote_copy(
                src_ref=gout.at[0, p],
                dst_ref=gin.at[place, p],
                send_sem=bs_sem.at[0, p],
                recv_sem=br_sem.at[place, p],
                device_id={"ctx": me},
                device_id_type=MESH,
            ).wait_recv()

    def add(slot, place, p):
        acc[slot, p] = acc[slot, p] + gin[place, p].astype(jnp.float32)

    def step_b(p):
        if 0 <= p < kvl:
            brecv(0, p)
            brecv(1, p)
            add(2 * core, 0, p)
            add(2 + 2 * core, 1, p)
            gout[1, p] = acc[2, p].astype(jnp.bfloat16)
            bstart(2, p)

    def step_c(p):
        if 0 <= p < kvl:
            brecv(2, p)
            add(4 * xpos, 2, p)
            gout[3, p] = acc[4, p].astype(jnp.bfloat16)
            bstart(4, p)

    def step_d(p):
        if 0 <= p < kvl:
            brecv(3, p)
            add(0, 3, p)

    def make_bias():
        q_docs = docs_row
        for k in range(slots):
            k_row = docs_row if k == 0 else buf[k, pl.ds(0, EXTRA), pl.ds(0, tokens)].astype(jnp.float32)[0:1]
            k_docs = jnp.transpose(jnp.broadcast_to(k_row, (tokens, tokens)))
            ok = k_docs == q_docs
            if k == 0:
                ok = ok & (
                    lax.broadcasted_iota(jnp.int32, (tokens, tokens), 0)
                    <= lax.broadcasted_iota(jnp.int32, (tokens, tokens), 1)
                )
            off = jnp.float32(-1e38)
            shown = jnp.where(ok, jnp.float32(0.0), off)
            if k > 0:
                shown = jnp.where(me >= k, shown, off)
            bias[pl.ds(k * tokens, tokens), :] = shown

    def attend(p):
        k_all = buf[:, rows_of(p), pl.ds(0, HEAD)].reshape(width, HEAD)
        v_all = buf[:, rows_of(p), pl.ds(HEAD, HEAD)].reshape(width, HEAD)
        v_t = jnp.transpose(v_all)
        q_rows, t_rows = [], []
        for j in range(GROUP // 2):
            base = (p * GROUP + 2 * j) * HEAD
            qs = [q_v[:, pl.ds(base + i * HEAD, HEAD)] for i in range(2)]
            ts = [t_v[:, pl.ds(base + i * HEAD, HEAD)] for i in range(2)]
            q2 = jnp.concatenate(qs, 0)
            t2 = jnp.concatenate(ts, 0)
            q_rows.append(q2)
            t_rows.append(t2)
            s = lax.dot_general(k_all, q2, NT, preferred_element_type=jnp.float32)
            dp = lax.dot_general(v_all, t2, NT, preferred_element_type=jnp.float32)
            b = bias[...]
            s = s + jnp.concatenate([b, b], 1)
            top = jnp.max(s, 0, keepdims=True)
            e = jnp.exp2((s - top) * coef)
            inv = 1.0 / jnp.sum(e, 0, keepdims=True)
            delta = jnp.sum(e * dp, 0, keepdims=True) * inv
            prob = e * inv
            p16 = prob.astype(jnp.bfloat16)
            cols = pl.ds(j * 2 * tokens, 2 * tokens)
            p_all[:, cols] = p16
            ds_all[:, cols] = (prob * (dp - delta)).astype(jnp.bfloat16)
            o_t = jnp.dot(v_t, p16, preferred_element_type=jnp.float32)
            out = jnp.transpose(o_t).astype(jnp.bfloat16)
            for i in range(2):
                o_v[:, pl.ds(base + i * HEAD, HEAD)] = out[i * tokens : (i + 1) * tokens]
        q_head = jnp.concatenate(q_rows, 0)
        t_head = jnp.concatenate(t_rows, 0)
        for part, (left, right, mult) in enumerate(((ds_all, q_head, scale), (p_all, t_head, 1.0))):
            grad = jnp.dot(left[...], right, preferred_element_type=jnp.float32)
            if mult != 1.0:
                grad = grad * mult
            cols = pl.ds(part * HEAD, HEAD)
            for k in range(slots):
                block = grad[k * tokens : (k + 1) * tokens]
                if k == 0 or (tree and k % 2 == 0):
                    acc[k, p, :, cols] = block
                else:
                    gout[k - 1, p, :, cols] = block.astype(jnp.bfloat16)

    def out_copy(p):
        cols = pl.ds(p * GROUP * HEAD, GROUP * HEAD)
        return pltpu.make_async_copy(o_v.at[:, cols], attn_hbm.at[:, cols], out_sem.at[p])

    relay4(0)
    relay4(1)
    relay2(0)
    for p in range(kvl):
        relay4(p + 2)
        relay2(p + 1)
        for k in range(1, slots):
            if not (tree and k % 2 == 0):
                frecv(k, p)
        if p == 0:
            make_bias()
            for copy in loads:
                copy.wait()
        attend(p)
        out_copy(p).start()
        if tree:
            bstart(1, p)
            bstart(3, p)
            step_b(p - 1)
            step_c(p - 2)
            step_d(p - 3)
        else:
            for k in range(1, slots):
                bstart(k, p)
    if tree:
        for p in range(kvl, kvl + 3):
            step_b(p - 1)
            step_c(p - 2)
            step_d(p - 3)
    else:
        for p in range(kvl):
            for i in range(reach):
                brecv(i, p)
                add(0, i, p)

    a_sum = jnp.zeros((tokens, LANES), jnp.float32)
    b_sum = jnp.zeros((tokens, LANES), jnp.float32)
    c_sum = jnp.zeros((tokens, LANES), jnp.float32)
    for p in range(kvl):
        cols = pl.ds(p * HEAD, HEAD)
        for part, ref in enumerate((ks_ref, vs_ref)):
            old = ref[:, cols]
            g = acc[0, p, :, pl.ds(part * HEAD, HEAD)]
            a_sum += old * old
            b_sum += old * g
            c_sum += g * g
    lane = lax.broadcasted_iota(jnp.int32, (tokens, LANES), 1)
    mixed = jnp.where(
        lane == 0,
        jnp.sum(a_sum, 1, keepdims=True),
        jnp.where(
            lane == 1,
            jnp.sum(b_sum, 1, keepdims=True),
            jnp.where(lane == 2, jnp.sum(c_sum, 1, keepdims=True), 0.0),
        ),
    )
    stat_mine[...] = jnp.transpose(mixed)[0:8]

    def stat_send(d):
        return pltpu.make_async_remote_copy(
            src_ref=stat_mine,
            dst_ref=stat_in.at[d - 1],
            send_sem=ss_sem,
            recv_sem=sr_sem,
            device_id=device_of(lax.rem(lin + d, total_dev)),
            device_id_type=MESH,
        )

    @pl.loop(1, total_dev)
    def _(d):
        stat_send(d).start()

    for p in range(kvl):
        out_copy(p).wait()
        for m in range(len(forward)):
            valid, src, target, slot = forward[m]
            @pl.when(valid)
            def _(m=m, p=p, src=src, target=target, slot=slot):
                fsend(m, p, src, target, slot).wait_send()
        for k in backward:
            @pl.when(backward[k][0])
            def _(k=k, p=p):
                bsend(k, p).wait_send()

    everything = pltpu.make_async_copy(stat_in, stat_in, sr_sem)
    everything.wait()
    pltpu.make_async_copy(stat_in, stat_in, ss_sem).wait()

    mine = stat_mine[...]
    whole = mine + jnp.sum(stat_in[...], 0)
    overall = jnp.sum(whole[2:3], 1, keepdims=True)
    count = n_dp * n * tokens * 2 * KV_HEADS * HEAD
    rate = step_size / jnp.sqrt(overall / count + 1e-05)
    rows = mine
    for d in range(1, n_tp):
        tp = lax.axis_index("tp")
        peer = lin - tp + lax.rem(tp + d, n_tp)
        away = lax.rem(lin - peer + total_dev, total_dev)
        rows = rows + stat_in[away - 1]
    size_sq = jnp.maximum(rows[0:1] + 2.0 * rate * rows[1:2] + rate * rate * rows[2:3], 0.0)
    radius = radius_scale * math.sqrt(2 * KV_HEADS * HEAD)
    factor = jnp.minimum(1.0, radius / jnp.sqrt(size_sq + 1e-06))
    factor_col = jnp.transpose(jnp.broadcast_to(factor, (LANES, tokens)))
    for p in range(kvl):
        cols = pl.ds(p * HEAD, HEAD)
        nks_ref[:, cols] = (ks_ref[:, cols] + rate * acc[0, p, :, pl.ds(0, HEAD)]) * factor_col
        nvs_ref[:, cols] = (vs_ref[:, cols] + rate * acc[0, p, :, pl.ds(HEAD, HEAD)]) * factor_col


def per_device(sizes, query, key, value, key_shift, value_shift, doc_ids, target):
    n_dp, n, n_tp = sizes
    tokens = query.shape[1]
    kvl = key.shape[2] // HEAD
    channels = query.shape[2]
    seq_total = tokens * n
    doc_limit = min(2048, seq_total // 4)
    reach = (doc_limit + tokens - 2) // tokens
    slots = reach + 1
    width = slots * tokens
    tree = reach == 4 and n % 4 == 0
    places = 4 if tree else reach
    total_dev = n_dp * n * n_tp
    cfg = (n_dp, n, n_tp, reach, kvl, tokens, tree)
    bf, f32 = jnp.bfloat16, jnp.float32
    vmem = pl.BlockSpec(memory_space=pltpu.VMEM)
    anyw = pl.BlockSpec(memory_space=pl.ANY)
    dma = pltpu.SemaphoreType.DMA
    attn, nks, nvs = pl.pallas_call(
        functools.partial(kernel, cfg),
        out_shape=(
            jax.ShapeDtypeStruct((tokens, channels), bf),
            jax.ShapeDtypeStruct((tokens, kvl * HEAD), f32),
            jax.ShapeDtypeStruct((tokens, kvl * HEAD), f32),
        ),
        in_specs=[anyw, anyw, vmem, vmem, vmem, vmem, vmem],
        out_specs=(anyw, vmem, vmem),
        scratch_shapes=[
            pltpu.VMEM((tokens, channels), bf),
            pltpu.VMEM((tokens, channels), bf),
            pltpu.VMEM((tokens, channels), bf),
            pltpu.VMEM((slots, EXTRA + kvl * tokens, 2 * HEAD), bf),
            pltpu.VMEM((width, tokens), f32),
            pltpu.VMEM((width, GROUP * tokens), bf),
            pltpu.VMEM((width, GROUP * tokens), bf),
            pltpu.VMEM((slots if tree else 1, kvl, tokens, 2 * HEAD), f32),
            pltpu.VMEM((reach, kvl, tokens, 2 * HEAD), bf),
            pltpu.VMEM((places, kvl, tokens, 2 * HEAD), bf),
            pltpu.VMEM((8, LANES), f32),
            pltpu.VMEM((total_dev - 1, 8, LANES), f32),
            dma((2,)),
            dma((kvl,)),
            dma((reach, kvl)),
            dma((reach, kvl)),
            dma((reach, kvl)),
            dma((places, kvl)),
            dma,
            dma,
        ],
        compiler_params=pltpu.CompilerParams(
            collective_id=0, has_side_effects=True, vmem_limit_bytes=56 * 1024 * 1024
        ),
    )(query[0], target[0], key[0], value[0], key_shift[0], value_shift[0], doc_ids)
    return attn[None], nks[None], nvs[None]


def solution(mesh):
    sizes = (mesh.shape["dp"], mesh.shape["ctx"], mesh.shape["tp"])
    wide = P("dp", "ctx", "tp")
    return jax.shard_map(
        functools.partial(per_device, sizes),
        mesh=mesh,
        in_specs=(wide, wide, wide, wide, wide, P("dp", "ctx"), wide),
        out_specs=(wide, wide, wide),
        check_vma=False,
    )
```

```python
import functools
import math

import jax
import jax.numpy as jnp
from jax import lax
from jax.experimental import pallas as pl
from jax.experimental.pallas import tpu as pltpu
from jax.sharding import PartitionSpec as P

HEADS = 64
KV_HEADS = 8
HEAD = 128
GROUP = HEADS // KV_HEADS
EXTRA = 16
LANES = 128

step_size = 0.1
radius_scale = 0.13

MESH = pl.DeviceIdType.MESH
NT = (((1,), (1,)), ((), ()))


def kernel(
    cfg,
    q_hbm, t_hbm, key_ref, value_ref, ks_ref, vs_ref, doc_ref,
    attn_hbm, grad_hbm, stat_ref,
    q_v, t_v, o_v, q_t, t_t, buf, bias, acc, gout, gin, stat_mine, stat_in,
    load_sem, out_sem, fs_sem, fr_sem, bs_sem, br_sem, ss_sem, sr_sem,
):
    n_dp, n, n_tp, reach, kvl, tokens, tree = cfg
    total_dev = n_dp * n * n_tp
    slots = reach + 1
    width = slots * tokens
    scale = 1.0 / math.sqrt(HEAD)
    coef = scale * math.log2(math.e)
    me = lax.axis_index("ctx")
    core = lax.rem(me, 2)
    xpos = lax.rem(me // 2, 2)
    mate = me + 1 - 2 * core

    my_dp, my_tp = lax.axis_index("dp"), lax.axis_index("tp")

    def wrap(index, size):
        return jnp.where(index >= size, index - size, index)

    def to_others(fn):
        for a in range(n_dp):
            for b in range(n_tp):
                def one(c, a=a, b=b):
                    place = (a * n_tp + b) * n + c
                    fn(
                        place - 1,
                        {"dp": wrap(my_dp + a, n_dp), "ctx": wrap(me + c, n), "tp": wrap(my_tp + b, n_tp)},
                    )
                first = 1 if a == 0 and b == 0 else 0
                if total_dev <= 64:
                    for c in range(first, n):
                        one(c)
                else:
                    pl.loop(first, n)(one)

    barrier = pltpu.get_barrier_semaphore()
    to_others(
        lambda place, device: pl.semaphore_signal(
            barrier, inc=1, device_id=device, device_id_type=MESH
        )
    )

    loads = [
        pltpu.make_async_copy(q_hbm, q_v, load_sem.at[0]),
        pltpu.make_async_copy(t_hbm, t_v, load_sem.at[1]),
    ]
    for copy in loads:
        copy.start()

    def rows_of(p):
        return pl.ds(EXTRA + p * tokens, tokens)

    def piece(p):
        return pl.ds(0, EXTRA + tokens) if p == 0 else rows_of(p)

    docs_row = doc_ref[...].astype(jnp.float32)
    buf[0, pl.ds(0, EXTRA), pl.ds(0, tokens)] = jnp.broadcast_to(docs_row, (EXTRA, tokens)).astype(
        jnp.bfloat16
    )
    buf[0, pl.ds(0, EXTRA), pl.ds(HEAD, HEAD)] = jnp.zeros((EXTRA, HEAD), jnp.bfloat16)
    for p in range(kvl):
        cols = pl.ds(p * HEAD, HEAD)
        buf[0, rows_of(p), pl.ds(0, HEAD)] = (
            key_ref[:, cols].astype(jnp.float32) + ks_ref[:, cols]
        ).astype(jnp.bfloat16)
        buf[0, rows_of(p), pl.ds(HEAD, HEAD)] = (
            value_ref[:, cols].astype(jnp.float32) + vs_ref[:, cols]
        ).astype(jnp.bfloat16)
    for k in range(1, slots):
        @pl.when(me < k)
        def _(k=k):
            buf[k] = jnp.zeros(buf.shape[1:], buf.dtype)

    has = {k: me >= k for k in range(1, slots)}

    def fsend(m, p, src, target, slot):
        return pltpu.make_async_remote_copy(
            src_ref=buf.at[src, piece(p)],
            dst_ref=buf.at[slot, piece(p)],
            send_sem=fs_sem.at[m, p],
            recv_sem=fr_sem.at[slot - 1, p],
            device_id={"ctx": target},
            device_id_type=MESH,
        )

    def frecv(slot, p):
        @pl.when(has[slot])
        def _():
            fsend(0, p, 0, me, slot).wait_recv()

    if tree:
        back_in = {
            0: (core == 0) | (me >= 3),
            1: ((core == 0) & (me >= 2)) | (me >= 5),
            2: (xpos == 0) | (me >= 4),
            3: me + 4 < n,
        }
        forward = [
            (me + 4 < n, 0, me + 4, 4),
            ((xpos == 0) | (me >= 4), 4 * xpos, me + 2 - 4 * xpos, 2),
            ((core == 0) | (me >= 2), 2 * core, mate, 1),
            (me >= 2 + 2 * core, 2 + 2 * core, mate, 3),
        ]
        backward = {
            1: (me >= 1, mate, 0),
            3: (me >= 3, mate, 1),
            2: (me >= 2, me + 2 - 4 * xpos, 2),
            4: (me >= 4, me - 4, 3),
        }
    else:
        back_in = {k - 1: me + k < n for k in range(1, slots)}
        forward = [(me + k < n, 0, me + k, k) for k in range(1, slots)]
        backward = {k: (me >= k, me - k, k - 1) for k in range(1, slots)}

    def fstart(m, p, extra=None):
        valid, src, target, slot = forward[m]
        @pl.when(valid if extra is None else valid & extra)
        def _():
            fsend(m, p, src, target, slot).start()

    for i in back_in:
        @pl.when(jnp.logical_not(back_in[i]))
        def _(i=i):
            gin[i] = jnp.zeros(gin.shape[1:], gin.dtype)

    pl.semaphore_wait(barrier, total_dev - 1)

    for p in range(kvl):
        if tree:
            fstart(0, p)
            fstart(1, p, xpos == 0)
            fstart(2, p, core == 0)
        else:
            for m in range(reach):
                fstart(m, p)

    def relay4(p):
        if tree and p < kvl:
            frecv(4, p)
            fstart(1, p, xpos == 1)

    def relay2(p):
        if tree and p < kvl:
            frecv(2, p)
            fstart(2, p, core == 1)
            fstart(3, p)

    def bsend(k, p):
        valid, target, place = backward[k]
        return pltpu.make_async_remote_copy(
            src_ref=gout.at[k - 1, p],
            dst_ref=gin.at[place, p],
            send_sem=bs_sem.at[k - 1, p],
            recv_sem=br_sem.at[place, p],
            device_id={"ctx": target},
            device_id_type=MESH,
        )

    def bstart(k, p):
        @pl.when(backward[k][0])
        def _():
            bsend(k, p).start()

    def brecv(place, p):
        @pl.when(back_in[place])
        def _():
            pltpu.make_async_remote_copy(
                src_ref=gout.at[0, p],
                dst_ref=gin.at[place, p],
                send_sem=bs_sem.at[0, p],
                recv_sem=br_sem.at[place, p],
                device_id={"ctx": me},
                device_id_type=MESH,
            ).wait_recv()

    def add(slot, place, p):
        acc[slot, p] = acc[slot, p] + gin[place, p].astype(jnp.float32)

    def step_b(p):
        if 0 <= p < kvl:
            brecv(0, p)
            brecv(1, p)
            add(2 * core, 0, p)
            add(2 + 2 * core, 1, p)
            gout[1, p] = acc[2, p].astype(jnp.bfloat16)
            bstart(2, p)

    def step_c(p):
        if 0 <= p < kvl:
            brecv(2, p)
            add(4 * xpos, 2, p)
            gout[3, p] = acc[4, p].astype(jnp.bfloat16)
            bstart(4, p)

    def step_d(p):
        if 0 <= p < kvl:
            brecv(3, p)
            add(0, 3, p)

    def make_bias():
        q_docs = docs_row
        for k in range(slots):
            k_row = docs_row if k == 0 else buf[k, pl.ds(0, EXTRA), pl.ds(0, tokens)].astype(jnp.float32)[0:1]
            k_docs = jnp.transpose(jnp.broadcast_to(k_row, (tokens, tokens)))
            ok = k_docs == q_docs
            if k == 0:
                ok = ok & (
                    lax.broadcasted_iota(jnp.int32, (tokens, tokens), 0)
                    <= lax.broadcasted_iota(jnp.int32, (tokens, tokens), 1)
                )
            off = jnp.float32(-1e38)
            shown = jnp.where(ok, jnp.float32(0.0), off)
            if k > 0:
                shown = jnp.where(me >= k, shown, off)
            bias[pl.ds(k * tokens, tokens), :] = shown

    def turn(p):
        for j in range(GROUP):
            here = pl.ds((p * GROUP + j) * HEAD, HEAD)
            cols = pl.ds(j * tokens, tokens)
            q_t[p, :, cols] = jnp.transpose(q_v[:, here])
            t_t[p, :, cols] = jnp.transpose(t_v[:, here])

    def attend(p):
        k_all = buf[:, rows_of(p), pl.ds(0, HEAD)].reshape(width, HEAD)
        v_all = buf[:, rows_of(p), pl.ds(HEAD, HEAD)].reshape(width, HEAD)
        v_t = jnp.transpose(v_all)
        pairs = GROUP // 2

        def products(j):
            cols = pl.ds(j * 2 * tokens, 2 * tokens)
            s = jnp.dot(k_all, q_t[p, :, cols], preferred_element_type=jnp.float32)
            dp = jnp.dot(v_all, t_t[p, :, cols], preferred_element_type=jnp.float32)
            return s, dp

        grad_k = grad_v = None
        ready = products(0)
        for j in range(pairs):
            s, dp = ready
            if j + 1 < pairs:
                ready = products(j + 1)
            base = (p * GROUP + 2 * j) * HEAD
            q2 = jnp.concatenate([q_v[:, pl.ds(base + i * HEAD, HEAD)] for i in range(2)], 0)
            t2 = jnp.concatenate([t_v[:, pl.ds(base + i * HEAD, HEAD)] for i in range(2)], 0)
            b = bias[...]
            s = s + jnp.concatenate([b, b], 1)
            top = jnp.max(s, 0, keepdims=True)
            e = jnp.exp2((s - top) * coef)
            inv = 1.0 / jnp.sum(e, 0, keepdims=True)
            delta = jnp.sum(e * dp, 0, keepdims=True) * inv
            prob = e * inv
            p16 = prob.astype(jnp.bfloat16)
            ds16 = (prob * (dp - delta)).astype(jnp.bfloat16)
            o_t = jnp.dot(v_t, p16, preferred_element_type=jnp.float32)
            out = jnp.transpose(o_t).astype(jnp.bfloat16)
            for i in range(2):
                o_v[:, pl.ds(base + i * HEAD, HEAD)] = out[i * tokens : (i + 1) * tokens]
            dk = jnp.dot(ds16, q2, preferred_element_type=jnp.float32)
            dv = jnp.dot(p16, t2, preferred_element_type=jnp.float32)
            grad_k = dk if j == 0 else grad_k + dk
            grad_v = dv if j == 0 else grad_v + dv
        for part, grad in enumerate((grad_k * scale, grad_v)):
            cols = pl.ds(part * HEAD, HEAD)
            for k in range(slots):
                block = grad[k * tokens : (k + 1) * tokens]
                if k == 0 or (tree and k % 2 == 0):
                    acc[k, p, :, cols] = block
                else:
                    gout[k - 1, p, :, cols] = block.astype(jnp.bfloat16)

    def out_copy(p):
        cols = pl.ds(p * GROUP * HEAD, GROUP * HEAD)
        return pltpu.make_async_copy(o_v.at[:, cols], attn_hbm.at[:, cols], out_sem.at[p])

    for copy in loads:
        copy.wait()
    turn(0)
    relay4(0)
    turn(1)
    relay4(1)
    relay2(0)
    for p in range(2, kvl):
        turn(p)
    for p in range(kvl):
        relay4(p + 2)
        relay2(p + 1)
        for k in range(1, slots):
            if not (tree and k % 2 == 0):
                frecv(k, p)
        if p == 0:
            make_bias()
        attend(p)
        out_copy(p).start()
        if tree:
            bstart(1, p)
            bstart(3, p)
            step_b(p - 1)
            step_c(p - 2)
            step_d(p - 3)
        else:
            for k in range(1, slots):
                bstart(k, p)
    if tree:
        for p in range(kvl, kvl + 3):
            step_b(p - 1)
            step_c(p - 2)
            step_d(p - 3)
    else:
        for p in range(kvl):
            for i in range(reach):
                brecv(i, p)
                add(0, i, p)

    a_sum = jnp.zeros((tokens, LANES), jnp.float32)
    b_sum = jnp.zeros((tokens, LANES), jnp.float32)
    c_sum = jnp.zeros((tokens, LANES), jnp.float32)
    for p in range(kvl):
        cols = pl.ds(p * HEAD, HEAD)
        for part, ref in enumerate((ks_ref, vs_ref)):
            old = ref[:, cols]
            g = acc[0, p, :, pl.ds(part * HEAD, HEAD)]
            a_sum += old * old
            b_sum += old * g
            c_sum += g * g
    lane = lax.broadcasted_iota(jnp.int32, (tokens, LANES), 1)
    mixed = jnp.where(
        lane == 0,
        jnp.sum(a_sum, 1, keepdims=True),
        jnp.where(
            lane == 1,
            jnp.sum(b_sum, 1, keepdims=True),
            jnp.where(lane == 2, jnp.sum(c_sum, 1, keepdims=True), 0.0),
        ),
    )
    stat_mine[...] = jnp.transpose(mixed)[0:8]

    def stat_send(place, device):
        pltpu.make_async_remote_copy(
            src_ref=stat_mine,
            dst_ref=stat_in.at[place],
            send_sem=ss_sem,
            recv_sem=sr_sem,
            device_id=device,
            device_id_type=MESH,
        ).start()

    to_others(stat_send)
    grad_copy = pltpu.make_async_copy(acc.at[0], grad_hbm, load_sem.at[0])
    grad_copy.start()

    for p in range(kvl):
        out_copy(p).wait()
        for m in range(len(forward)):
            valid, src, target, slot = forward[m]
            @pl.when(valid)
            def _(m=m, p=p, src=src, target=target, slot=slot):
                fsend(m, p, src, target, slot).wait_send()
        for k in backward:
            @pl.when(backward[k][0])
            def _(k=k, p=p):
                bsend(k, p).wait_send()

    everything = pltpu.make_async_copy(stat_in, stat_in, sr_sem)
    everything.wait()
    pltpu.make_async_copy(stat_in, stat_in, ss_sem).wait()

    mine = stat_mine[...]
    whole = mine + jnp.sum(stat_in[...], 0)
    overall = jnp.sum(whole[2:3], 1, keepdims=True)
    count = n_dp * n * tokens * 2 * KV_HEADS * HEAD
    rate = step_size / jnp.sqrt(overall / count + 1e-05)
    rows = mine
    for b in range(1, n_tp):
        rows = rows + stat_in[b * n - 1]
    size_sq = jnp.maximum(rows[0:1] + 2.0 * rate * rows[1:2] + rate * rate * rows[2:3], 0.0)
    radius = radius_scale * math.sqrt(2 * KV_HEADS * HEAD)
    factor = jnp.minimum(1.0, radius / jnp.sqrt(size_sq + 1e-06))
    grad_copy.wait()
    stat_ref[...] = jnp.where(
        lax.broadcasted_iota(jnp.int32, (8, LANES), 0) == 0, factor, jnp.broadcast_to(rate, (8, LANES))
    )


def finish(kvl, tokens, attn_in, grad_ref, stat_ref, ks_ref, vs_ref, attn_out, nks_ref, nvs_ref, sem):
    parts = 4
    wide = attn_in.shape[1] // parts
    copies = [
        pltpu.make_async_copy(
            attn_in.at[:, pl.ds(i * wide, wide)], attn_out.at[:, pl.ds(i * wide, wide)], sem.at[i]
        )
        for i in range(parts)
    ]
    for copy in copies:
        copy.start()
    factor = jnp.transpose(jnp.broadcast_to(stat_ref[0:1], (LANES, tokens)))
    rate = stat_ref[1:2]
    for p in range(kvl):
        cols = pl.ds(p * HEAD, HEAD)
        nks_ref[:, cols] = (ks_ref[:, cols] + rate * grad_ref[p, :, pl.ds(0, HEAD)]) * factor
        nvs_ref[:, cols] = (vs_ref[:, cols] + rate * grad_ref[p, :, pl.ds(HEAD, HEAD)]) * factor
    for copy in copies:
        copy.wait()


def per_device(sizes, query, key, value, key_shift, value_shift, doc_ids, target):
    n_dp, n, n_tp = sizes
    tokens = query.shape[1]
    kvl = key.shape[2] // HEAD
    channels = query.shape[2]
    seq_total = tokens * n
    doc_limit = min(2048, seq_total // 4)
    reach = (doc_limit + tokens - 2) // tokens
    slots = reach + 1
    width = slots * tokens
    tree = reach == 4 and n % 4 == 0
    places = 4 if tree else reach
    total_dev = n_dp * n * n_tp
    cfg = (n_dp, n, n_tp, reach, kvl, tokens, tree)
    bf, f32 = jnp.bfloat16, jnp.float32
    vmem = pl.BlockSpec(memory_space=pltpu.VMEM)
    anyw = pl.BlockSpec(memory_space=pl.ANY)
    dma = pltpu.SemaphoreType.DMA
    attn, grads, stats = pl.pallas_call(
        functools.partial(kernel, cfg),
        out_shape=(
            jax.ShapeDtypeStruct((tokens, channels), bf),
            jax.ShapeDtypeStruct((kvl, tokens, 2 * HEAD), f32),
            jax.ShapeDtypeStruct((8, LANES), f32),
        ),
        in_specs=[anyw, anyw, vmem, vmem, vmem, vmem, vmem],
        out_specs=(anyw, anyw, vmem),
        scratch_shapes=[
            pltpu.VMEM((tokens, channels), bf),
            pltpu.VMEM((tokens, channels), bf),
            pltpu.VMEM((tokens, channels), bf),
            pltpu.VMEM((kvl, HEAD, GROUP * tokens), bf),
            pltpu.VMEM((kvl, HEAD, GROUP * tokens), bf),
            pltpu.VMEM((slots, EXTRA + kvl * tokens, 2 * HEAD), bf),
            pltpu.VMEM((width, tokens), f32),
            pltpu.VMEM((slots if tree else 1, kvl, tokens, 2 * HEAD), f32),
            pltpu.VMEM((reach, kvl, tokens, 2 * HEAD), bf),
            pltpu.VMEM((places, kvl, tokens, 2 * HEAD), bf),
            pltpu.VMEM((8, LANES), f32),
            pltpu.VMEM((total_dev - 1, 8, LANES), f32),
            dma((2,)),
            dma((kvl,)),
            dma((reach, kvl)),
            dma((reach, kvl)),
            dma((reach, kvl)),
            dma((places, kvl)),
            dma,
            dma,
        ],
        compiler_params=pltpu.CompilerParams(
            collective_id=0, has_side_effects=True, vmem_limit_bytes=60 * 1024 * 1024
        ),
    )(query[0], target[0], key[0], value[0], key_shift[0], value_shift[0], doc_ids)
    attn, nks, nvs = pl.pallas_call(
        functools.partial(finish, kvl, tokens),
        out_shape=(
            jax.ShapeDtypeStruct((tokens, channels), bf),
            jax.ShapeDtypeStruct((tokens, kvl * HEAD), f32),
            jax.ShapeDtypeStruct((tokens, kvl * HEAD), f32),
        ),
        in_specs=[anyw, vmem, vmem, vmem, vmem],
        out_specs=(anyw, vmem, vmem),
        scratch_shapes=[dma((4,))],
        compiler_params=pltpu.CompilerParams(vmem_limit_bytes=60 * 1024 * 1024),
    )(attn, grads, stats, key_shift[0], value_shift[0])
    return attn[None], nks[None], nvs[None]


def solution(mesh):
    sizes = (mesh.shape["dp"], mesh.shape["ctx"], mesh.shape["tp"])
    wide = P("dp", "ctx", "tp")
    return jax.shard_map(
        functools.partial(per_device, sizes),
        mesh=mesh,
        in_specs=(wide, wide, wide, wide, wide, P("dp", "ctx"), wide),
        out_specs=(wide, wide, wide),
        check_vma=False,
    )
```

```python
import functools
import math

import jax
import jax.numpy as jnp
from jax import lax
from jax.experimental import pallas as pl
from jax.experimental.pallas import tpu as pltpu
from jax.sharding import PartitionSpec as P

HEADS = 64
KV_HEADS = 8
HEAD = 128
GROUP = HEADS // KV_HEADS
EXTRA = 16
LANES = 128

step_size = 0.1
radius_scale = 0.13

MESH = pl.DeviceIdType.MESH
NT = (((1,), (1,)), ((), ()))


def kernel(
    cfg,
    q_hbm, t_hbm, key_hbm, value_hbm, ks_hbm, vs_hbm, doc_ref,
    attn_hbm, grad_hbm, stat_ref,
    key_ref, value_ref, ks_ref, vs_ref,
    q_v, t_v, o_v, q_t, t_t, e_own, dp_own, row_own, buf, bias, acc, gout, gin, stat_mine, stat_in,
    load_sem, out_sem, fs_sem, fr_sem, bs_sem, br_sem, ss_sem, sr_sem,
):
    n_dp, n, n_tp, reach, kvl, tokens, tree = cfg
    total_dev = n_dp * n * n_tp
    slots = reach + 1
    width = slots * tokens
    scale = 1.0 / math.sqrt(HEAD)
    coef = scale * math.log2(math.e)
    me = lax.axis_index("ctx")
    core = lax.rem(me, 2)
    xpos = lax.rem(me // 2, 2)
    mate = me + 1 - 2 * core

    my_dp, my_tp = lax.axis_index("dp"), lax.axis_index("tp")

    def wrap(index, size):
        return jnp.where(index >= size, index - size, index)

    def to_others(fn):
        for a in range(n_dp):
            for b in range(n_tp):
                def one(c, a=a, b=b):
                    place = (a * n_tp + b) * n + c
                    fn(
                        place - 1,
                        {"dp": wrap(my_dp + a, n_dp), "ctx": wrap(me + c, n), "tp": wrap(my_tp + b, n_tp)},
                    )
                first = 1 if a == 0 and b == 0 else 0
                if total_dev <= 64:
                    for c in range(first, n):
                        one(c)
                else:
                    pl.loop(first, n)(one)

    small = [
        pltpu.make_async_copy(src, dst, load_sem.at[2 + i])
        for i, (src, dst) in enumerate(
            ((key_hbm, key_ref), (ks_hbm, ks_ref), (value_hbm, value_ref), (vs_hbm, vs_ref))
        )
    ]
    for copy in small:
        copy.start()
    barrier = pltpu.get_barrier_semaphore()
    to_others(
        lambda place, device: pl.semaphore_signal(
            barrier, inc=1, device_id=device, device_id_type=MESH
        )
    )

    loads = [
        pltpu.make_async_copy(q_hbm, q_v, load_sem.at[0]),
        pltpu.make_async_copy(t_hbm, t_v, load_sem.at[1]),
    ]
    for copy in loads:
        copy.start()

    def rows_of(p):
        return pl.ds(EXTRA + p * tokens, tokens)

    def piece(p):
        return pl.ds(0, EXTRA + tokens) if p == 0 else rows_of(p)

    docs_row = doc_ref[...].astype(jnp.float32)
    buf[0, pl.ds(0, EXTRA), pl.ds(0, tokens)] = jnp.broadcast_to(docs_row, (EXTRA, tokens)).astype(
        jnp.bfloat16
    )
    buf[0, pl.ds(0, EXTRA), pl.ds(HEAD, HEAD)] = jnp.zeros((EXTRA, HEAD), jnp.bfloat16)
    for copy in small:
        copy.wait()
    for p in range(kvl):
        cols = pl.ds(p * HEAD, HEAD)
        buf[0, rows_of(p), pl.ds(0, HEAD)] = (
            key_ref[:, cols].astype(jnp.float32) + ks_ref[:, cols]
        ).astype(jnp.bfloat16)
        buf[0, rows_of(p), pl.ds(HEAD, HEAD)] = (
            value_ref[:, cols].astype(jnp.float32) + vs_ref[:, cols]
        ).astype(jnp.bfloat16)
    for k in range(1, slots):
        @pl.when(me < k)
        def _(k=k):
            buf[k] = jnp.zeros(buf.shape[1:], buf.dtype)

    has = {k: me >= k for k in range(1, slots)}

    def fsend(m, p, src, target, slot):
        return pltpu.make_async_remote_copy(
            src_ref=buf.at[src, piece(p)],
            dst_ref=buf.at[slot, piece(p)],
            send_sem=fs_sem.at[m, p],
            recv_sem=fr_sem.at[slot - 1, p],
            device_id={"ctx": target},
            device_id_type=MESH,
        )

    def frecv(slot, p):
        @pl.when(has[slot])
        def _():
            fsend(0, p, 0, me, slot).wait_recv()

    if tree:
        back_in = {
            0: (core == 0) | (me >= 3),
            1: ((core == 0) & (me >= 2)) | (me >= 5),
            2: (xpos == 0) | (me >= 4),
            3: me + 4 < n,
        }
        forward = [
            (me + 4 < n, 0, me + 4, 4),
            ((xpos == 0) | (me >= 4), 4 * xpos, me + 2 - 4 * xpos, 2),
            ((core == 0) | (me >= 2), 2 * core, mate, 1),
            (me >= 2 + 2 * core, 2 + 2 * core, mate, 3),
        ]
        backward = {
            1: (me >= 1, mate, 0),
            3: (me >= 3, mate, 1),
            2: (me >= 2, me + 2 - 4 * xpos, 2),
            4: (me >= 4, me - 4, 3),
        }
    else:
        back_in = {k - 1: me + k < n for k in range(1, slots)}
        forward = [(me + k < n, 0, me + k, k) for k in range(1, slots)]
        backward = {k: (me >= k, me - k, k - 1) for k in range(1, slots)}

    def fstart(m, p, extra=None):
        valid, src, target, slot = forward[m]
        @pl.when(valid if extra is None else valid & extra)
        def _():
            fsend(m, p, src, target, slot).start()

    for i in back_in:
        @pl.when(jnp.logical_not(back_in[i]))
        def _(i=i):
            gin[i] = jnp.zeros(gin.shape[1:], gin.dtype)

    pl.semaphore_wait(barrier, total_dev - 1)

    def first_sends(p):
        if tree:
            fstart(0, p)
            fstart(1, p, xpos == 0)
            fstart(2, p, core == 0)
        else:
            for m in range(reach):
                fstart(m, p)

    first_sends(0)

    def relay4(p):
        if tree and p < kvl:
            frecv(4, p)
            fstart(1, p, xpos == 1)

    def relay2(p):
        if tree and p < kvl:
            frecv(2, p)
            fstart(2, p, core == 1)
            fstart(3, p)

    def bsend(k, p):
        valid, target, place = backward[k]
        return pltpu.make_async_remote_copy(
            src_ref=gout.at[k - 1, p],
            dst_ref=gin.at[place, p],
            send_sem=bs_sem.at[k - 1, p],
            recv_sem=br_sem.at[place, p],
            device_id={"ctx": target},
            device_id_type=MESH,
        )

    def bstart(k, p):
        @pl.when(backward[k][0])
        def _():
            bsend(k, p).start()

    def brecv(place, p):
        @pl.when(back_in[place])
        def _():
            pltpu.make_async_remote_copy(
                src_ref=gout.at[0, p],
                dst_ref=gin.at[place, p],
                send_sem=bs_sem.at[0, p],
                recv_sem=br_sem.at[place, p],
                device_id={"ctx": me},
                device_id_type=MESH,
            ).wait_recv()

    def add(slot, place, p):
        acc[slot, p] = acc[slot, p] + gin[place, p].astype(jnp.float32)

    def step_b(p):
        if 0 <= p < kvl:
            brecv(0, p)
            brecv(1, p)
            add(2 * core, 0, p)
            add(2 + 2 * core, 1, p)
            gout[1, p] = acc[2, p].astype(jnp.bfloat16)
            bstart(2, p)

    def step_c(p):
        if 0 <= p < kvl:
            brecv(2, p)
            add(4 * xpos, 2, p)
            gout[3, p] = acc[4, p].astype(jnp.bfloat16)
            bstart(4, p)

    def step_d(p):
        if 0 <= p < kvl:
            brecv(3, p)
            add(0, 3, p)

    off = jnp.float32(-1e38)

    def own_bias():
        ok = (jnp.transpose(jnp.broadcast_to(docs_row, (tokens, tokens))) == docs_row) & (
            lax.broadcasted_iota(jnp.int32, (tokens, tokens), 0)
            <= lax.broadcasted_iota(jnp.int32, (tokens, tokens), 1)
        )
        bias[pl.ds(0, tokens), :] = jnp.where(ok, jnp.float32(0.0), off)

    def make_bias():
        for k in range(1, slots):
            k_row = buf[k, pl.ds(0, EXTRA), pl.ds(0, tokens)].astype(jnp.float32)[0:1]
            ok = jnp.transpose(jnp.broadcast_to(k_row, (tokens, tokens))) == docs_row
            shown = jnp.where(ok, jnp.float32(0.0), off)
            bias[pl.ds(k * tokens, tokens), :] = jnp.where(me >= k, shown, off)

    def own_part(p):
        k_own = buf[0, rows_of(p), pl.ds(0, HEAD)]
        v_own = buf[0, rows_of(p), pl.ds(HEAD, HEAD)]
        b = bias[pl.ds(0, tokens), :]
        b2 = jnp.concatenate([b, b], 1)
        for j in range(GROUP // 2):
            cols = pl.ds(j * 2 * tokens, 2 * tokens)
            s = jnp.dot(k_own, q_t[p, :, cols], preferred_element_type=jnp.float32) + b2
            dp = jnp.dot(v_own, t_t[p, :, cols], preferred_element_type=jnp.float32)
            top = jnp.max(s, 0, keepdims=True)
            e = jnp.exp2((s - top) * coef)
            e_own[p, :, cols] = e
            dp_own[p, :, cols] = dp
            row_own[p, pl.ds(0, 1), cols] = top
            row_own[p, pl.ds(1, 1), cols] = jnp.sum(e, 0, keepdims=True)
            row_own[p, pl.ds(2, 1), cols] = jnp.sum(e * dp, 0, keepdims=True)

    def turn(p):
        for j in range(GROUP):
            here = pl.ds((p * GROUP + j) * HEAD, HEAD)
            cols = pl.ds(j * tokens, tokens)
            q_t[p, :, cols] = jnp.transpose(q_v[:, here])
            t_t[p, :, cols] = jnp.transpose(t_v[:, here])

    def attend(p):
        k_past = buf[pl.ds(1, reach), rows_of(p), pl.ds(0, HEAD)].reshape(reach * tokens, HEAD)
        v_all = buf[:, rows_of(p), pl.ds(HEAD, HEAD)].reshape(width, HEAD)
        v_past = v_all[tokens:]
        v_t = jnp.transpose(v_all)
        pairs = GROUP // 2

        def products(j):
            cols = pl.ds(j * 2 * tokens, 2 * tokens)
            s = jnp.dot(k_past, q_t[p, :, cols], preferred_element_type=jnp.float32)
            dp = jnp.dot(v_past, t_t[p, :, cols], preferred_element_type=jnp.float32)
            return s, dp

        grad_k = grad_v = None
        ready = products(0)
        for j in range(pairs):
            s, dp = ready
            if j + 1 < pairs:
                ready = products(j + 1)
            base = (p * GROUP + 2 * j) * HEAD
            q2 = jnp.concatenate([q_v[:, pl.ds(base + i * HEAD, HEAD)] for i in range(2)], 0)
            t2 = jnp.concatenate([t_v[:, pl.ds(base + i * HEAD, HEAD)] for i in range(2)], 0)
            cols = pl.ds(j * 2 * tokens, 2 * tokens)
            b = bias[pl.ds(tokens, reach * tokens), :]
            s = s + jnp.concatenate([b, b], 1)
            top_own = row_own[p, pl.ds(0, 1), cols]
            top = jnp.maximum(jnp.max(s, 0, keepdims=True), top_own)
            e = jnp.exp2((s - top) * coef)
            shrink = jnp.exp2((top_own - top) * coef)
            inv = 1.0 / (jnp.sum(e, 0, keepdims=True) + row_own[p, pl.ds(1, 1), cols] * shrink)
            delta = (
                jnp.sum(e * dp, 0, keepdims=True) + row_own[p, pl.ds(2, 1), cols] * shrink
            ) * inv
            prob = e * inv
            prob_own = e_own[p, :, cols] * (shrink * inv)
            ds_own = (prob_own * (dp_own[p, :, cols] - delta)).astype(jnp.bfloat16)
            p16 = jnp.concatenate([prob_own.astype(jnp.bfloat16), prob.astype(jnp.bfloat16)], 0)
            ds16 = jnp.concatenate([ds_own, (prob * (dp - delta)).astype(jnp.bfloat16)], 0)
            o_t = jnp.dot(v_t, p16, preferred_element_type=jnp.float32)
            out = jnp.transpose(o_t).astype(jnp.bfloat16)
            for i in range(2):
                o_v[:, pl.ds(base + i * HEAD, HEAD)] = out[i * tokens : (i + 1) * tokens]
            dk = jnp.dot(ds16, q2, preferred_element_type=jnp.float32)
            dv = jnp.dot(p16, t2, preferred_element_type=jnp.float32)
            grad_k = dk if j == 0 else grad_k + dk
            grad_v = dv if j == 0 else grad_v + dv
        for part, grad in enumerate((grad_k * scale, grad_v)):
            cols = pl.ds(part * HEAD, HEAD)
            for k in range(slots):
                block = grad[k * tokens : (k + 1) * tokens]
                if k == 0 or (tree and k % 2 == 0):
                    acc[k, p, :, cols] = block
                else:
                    gout[k - 1, p, :, cols] = block.astype(jnp.bfloat16)

    def out_copy(p):
        cols = pl.ds(p * GROUP * HEAD, GROUP * HEAD)
        return pltpu.make_async_copy(o_v.at[:, cols], attn_hbm.at[:, cols], out_sem.at[p])

    own_bias()
    for copy in loads:
        copy.wait()
    for p in range(kvl):
        turn(p)
        if p + 1 < kvl:
            first_sends(p + 1)
        own_part(p)
        if p < 2:
            relay4(p)
        if p == 1:
            relay2(0)
    for p in range(kvl):
        relay4(p + 2)
        relay2(p + 1)
        for k in range(1, slots):
            if not (tree and k % 2 == 0):
                frecv(k, p)
        if p == 0:
            make_bias()
        attend(p)
        out_copy(p).start()
        if tree:
            bstart(1, p)
            bstart(3, p)
            step_b(p - 1)
            step_c(p - 2)
            step_d(p - 3)
        else:
            for k in range(1, slots):
                bstart(k, p)
    if tree:
        for p in range(kvl, kvl + 3):
            step_b(p - 1)
            step_c(p - 2)
            step_d(p - 3)
    else:
        for p in range(kvl):
            for i in range(reach):
                brecv(i, p)
                add(0, i, p)

    a_sum = jnp.zeros((tokens, LANES), jnp.float32)
    b_sum = jnp.zeros((tokens, LANES), jnp.float32)
    c_sum = jnp.zeros((tokens, LANES), jnp.float32)
    for p in range(kvl):
        cols = pl.ds(p * HEAD, HEAD)
        for part, ref in enumerate((ks_ref, vs_ref)):
            old = ref[:, cols]
            g = acc[0, p, :, pl.ds(part * HEAD, HEAD)]
            a_sum += old * old
            b_sum += old * g
            c_sum += g * g
    lane = lax.broadcasted_iota(jnp.int32, (tokens, LANES), 1)
    mixed = jnp.where(
        lane == 0,
        jnp.sum(a_sum, 1, keepdims=True),
        jnp.where(
            lane == 1,
            jnp.sum(b_sum, 1, keepdims=True),
            jnp.where(lane == 2, jnp.sum(c_sum, 1, keepdims=True), 0.0),
        ),
    )
    stat_mine[...] = jnp.transpose(mixed)[0:8]

    def stat_send(place, device):
        pltpu.make_async_remote_copy(
            src_ref=stat_mine,
            dst_ref=stat_in.at[place],
            send_sem=ss_sem,
            recv_sem=sr_sem,
            device_id=device,
            device_id_type=MESH,
        ).start()

    to_others(stat_send)
    grad_copy = pltpu.make_async_copy(acc.at[0], grad_hbm, load_sem.at[0])
    grad_copy.start()

    for p in range(kvl):
        out_copy(p).wait()
        for m in range(len(forward)):
            valid, src, target, slot = forward[m]
            @pl.when(valid)
            def _(m=m, p=p, src=src, target=target, slot=slot):
                fsend(m, p, src, target, slot).wait_send()
        for k in backward:
            @pl.when(backward[k][0])
            def _(k=k, p=p):
                bsend(k, p).wait_send()

    everything = pltpu.make_async_copy(stat_in, stat_in, sr_sem)
    everything.wait()
    pltpu.make_async_copy(stat_in, stat_in, ss_sem).wait()

    mine = stat_mine[...]
    whole = mine + jnp.sum(stat_in[...], 0)
    overall = jnp.sum(whole[2:3], 1, keepdims=True)
    count = n_dp * n * tokens * 2 * KV_HEADS * HEAD
    rate = step_size / jnp.sqrt(overall / count + 1e-05)
    rows = mine
    for b in range(1, n_tp):
        rows = rows + stat_in[b * n - 1]
    size_sq = jnp.maximum(rows[0:1] + 2.0 * rate * rows[1:2] + rate * rate * rows[2:3], 0.0)
    radius = radius_scale * math.sqrt(2 * KV_HEADS * HEAD)
    factor = jnp.minimum(1.0, radius / jnp.sqrt(size_sq + 1e-06))
    grad_copy.wait()
    stat_ref[...] = jnp.where(
        lax.broadcasted_iota(jnp.int32, (8, LANES), 0) == 0, factor, jnp.broadcast_to(rate, (8, LANES))
    )


def finish(
    kvl, tokens,
    attn_in, grad_in, stat_ref, ks_in, vs_in, attn_out, nks_out, nvs_out,
    held, grad_ref, ks_ref, vs_ref, nks_ref, nvs_ref, sem,
):
    parts = 4
    high = tokens // parts
    chunks = [pl.ds(i * high, high) for i in range(parts)]
    fetch = [pltpu.make_async_copy(attn_in.at[c], held.at[c], sem.at[i]) for i, c in enumerate(chunks)]
    copies = [
        pltpu.make_async_copy(held.at[c], attn_out.at[c], sem.at[parts + i])
        for i, c in enumerate(chunks)
    ]
    more = [
        pltpu.make_async_copy(src, dst, sem.at[2 * parts + i])
        for i, (src, dst) in enumerate(((grad_in, grad_ref), (ks_in, ks_ref), (vs_in, vs_ref)))
    ]
    stores = [
        pltpu.make_async_copy(src, dst, sem.at[2 * parts + 3 + i])
        for i, (src, dst) in enumerate(((nks_ref, nks_out), (nvs_ref, nvs_out)))
    ]
    for copy in fetch + more:
        copy.start()
    factor = jnp.transpose(jnp.broadcast_to(stat_ref[0:1], (LANES, tokens)))
    rate = stat_ref[1:2]
    for i in range(parts):
        fetch[i].wait()
        copies[i].start()
    for copy in more:
        copy.wait()
    for part, (old, new) in enumerate(((ks_ref, nks_ref), (vs_ref, nvs_ref))):
        for p in range(kvl):
            cols = pl.ds(p * HEAD, HEAD)
            new[:, cols] = (old[:, cols] + rate * grad_ref[p, :, pl.ds(part * HEAD, HEAD)]) * factor
        stores[part].start()
    for copy in copies + stores:
        copy.wait()


def per_device(sizes, query, key, value, key_shift, value_shift, doc_ids, target):
    n_dp, n, n_tp = sizes
    tokens = query.shape[1]
    kvl = key.shape[2] // HEAD
    channels = query.shape[2]
    seq_total = tokens * n
    doc_limit = min(2048, seq_total // 4)
    reach = (doc_limit + tokens - 2) // tokens
    slots = reach + 1
    width = slots * tokens
    tree = reach == 4 and n % 4 == 0
    places = 4 if tree else reach
    total_dev = n_dp * n * n_tp
    cfg = (n_dp, n, n_tp, reach, kvl, tokens, tree)
    bf, f32 = jnp.bfloat16, jnp.float32
    vmem = pl.BlockSpec(memory_space=pltpu.VMEM)
    anyw = pl.BlockSpec(memory_space=pl.ANY)
    dma = pltpu.SemaphoreType.DMA
    attn, grads, stats = pl.pallas_call(
        functools.partial(kernel, cfg),
        out_shape=(
            jax.ShapeDtypeStruct((tokens, channels), bf),
            jax.ShapeDtypeStruct((kvl, tokens, 2 * HEAD), f32),
            jax.ShapeDtypeStruct((8, LANES), f32),
        ),
        in_specs=[anyw, anyw, anyw, anyw, anyw, anyw, vmem],
        out_specs=(anyw, anyw, vmem),
        scratch_shapes=[
            pltpu.VMEM((tokens, kvl * HEAD), bf),
            pltpu.VMEM((tokens, kvl * HEAD), bf),
            pltpu.VMEM((tokens, kvl * HEAD), f32),
            pltpu.VMEM((tokens, kvl * HEAD), f32),
            pltpu.VMEM((tokens, channels), bf),
            pltpu.VMEM((tokens, channels), bf),
            pltpu.VMEM((tokens, channels), bf),
            pltpu.VMEM((kvl, HEAD, GROUP * tokens), bf),
            pltpu.VMEM((kvl, HEAD, GROUP * tokens), bf),
            pltpu.VMEM((kvl, tokens, GROUP * tokens), f32),
            pltpu.VMEM((kvl, tokens, GROUP * tokens), f32),
            pltpu.VMEM((kvl, 8, GROUP * tokens), f32),
            pltpu.VMEM((slots, EXTRA + kvl * tokens, 2 * HEAD), bf),
            pltpu.VMEM((width, tokens), f32),
            pltpu.VMEM((slots if tree else 1, kvl, tokens, 2 * HEAD), f32),
            pltpu.VMEM((reach, kvl, tokens, 2 * HEAD), bf),
            pltpu.VMEM((places, kvl, tokens, 2 * HEAD), bf),
            pltpu.VMEM((8, LANES), f32),
            pltpu.VMEM((total_dev - 1, 8, LANES), f32),
            dma((6,)),
            dma((kvl,)),
            dma((reach, kvl)),
            dma((reach, kvl)),
            dma((reach, kvl)),
            dma((places, kvl)),
            dma,
            dma,
        ],
        compiler_params=pltpu.CompilerParams(
            collective_id=0, has_side_effects=True, vmem_limit_bytes=60 * 1024 * 1024
        ),
    )(query[0], target[0], key[0], value[0], key_shift[0], value_shift[0], doc_ids)
    attn, nks, nvs = pl.pallas_call(
        functools.partial(finish, kvl, tokens),
        out_shape=(
            jax.ShapeDtypeStruct((tokens, channels), bf),
            jax.ShapeDtypeStruct((tokens, kvl * HEAD), f32),
            jax.ShapeDtypeStruct((tokens, kvl * HEAD), f32),
        ),
        in_specs=[anyw, anyw, vmem, anyw, anyw],
        out_specs=(anyw, anyw, anyw),
        scratch_shapes=[
            pltpu.VMEM((tokens, channels), bf),
            pltpu.VMEM((kvl, tokens, 2 * HEAD), f32),
            pltpu.VMEM((tokens, kvl * HEAD), f32),
            pltpu.VMEM((tokens, kvl * HEAD), f32),
            pltpu.VMEM((tokens, kvl * HEAD), f32),
            pltpu.VMEM((tokens, kvl * HEAD), f32),
            dma((13,)),
        ],
        compiler_params=pltpu.CompilerParams(vmem_limit_bytes=60 * 1024 * 1024),
    )(attn, grads, stats, key_shift[0], value_shift[0])
    return attn[None], nks[None], nvs[None]


def solution(mesh):
    sizes = (mesh.shape["dp"], mesh.shape["ctx"], mesh.shape["tp"])
    wide = P("dp", "ctx", "tp")
    return jax.shard_map(
        functools.partial(per_device, sizes),
        mesh=mesh,
        in_specs=(wide, wide, wide, wide, wide, P("dp", "ctx"), wide),
        out_specs=(wide, wide, wide),
        check_vma=False,
    )
```
